32 devices in a mesh: groups: 2 (over y), ep: 16 (over z, x, core).
Axes of the slice: x: 2, y: 2, z: 4, core: 2. Of those that a mesh axis runs over, the one named last changes fastest.
Arguments:
- queries: bfloat16 [64, 128, 576], P(('groups', 'ep')), parts along dimension 0, may hold values from -120 to 120
- kv_cache: bfloat16 [64, 256, 576], P(('groups', 'ep')), parts along dimension 0, may hold values from -6 to 6
- kv_lengths: int32 [64], P(('groups', 'ep')), parts along dimension 0, may hold values from 32 to 256, as said below
- moe_input: bfloat16 [64, 7168], P(('groups', 'ep')), parts along dimension 0, may hold values from -6 to 6
- expert_ids: int32 [64, 8], P(('groups', 'ep')), parts along dimension 0, may hold values from 0 to 15, all different within a row; in each aligned block of 2 rows (0 to 1, 2 to 3, ...) at most 2 rows name the same one
- route_weights: float32 [64, 8], P(('groups', 'ep')), parts along dimension 0, may hold values from 0.1 to 1
- w_gate: bfloat16 [32768, 7168], P('ep'), may hold values from -0.0625 to 0.0625
- w_up: bfloat16 [32768, 7168], P('ep'), may hold values from -0.0625 to 0.0625
- w_down: bfloat16 [32768, 7168], P('ep'), may hold values from -0.125 to 0.125
Outputs:
- attended: bfloat16 [64, 128, 512], P(('groups', 'ep')), parts along dimension 0
- moe_output: bfloat16 [64, 7168], P(('groups', 'ep')), parts along dimension 0
The draws below stay inside these ranges and needn't reach their ends.
There are 2 independent parts, one for each index of `groups`. The reference program is written for one: setup_inputs(seed, part) draws one part's arguments, and reference() takes and returns one part's arrays. A program takes and returns all parts, laid end to end along the dimension named above; an argument that names none is the same for every part. Nothing has to cross between parts.
Inputs may be any that keep to these rules, and one draw needn't show every extreme that they name: `expert_ids`: the 8 ids of a row differ. Among the 2 rows of one device no expert is named more than 2 times, and in every draw some expert is named exactly 2 times by the rows of some device. `kv_lengths`: some request in every draw uses all 256 slots.
All inputs are finite; a program needn't handle non-finite values.
Results may differ from the reference program's by a relative error of at most 0.0085.
Values may be sent and summed in bfloat16 or wider, within the bound.
A program may use at most 128 MiB of HBM per device.

```python
import math
import jax
import jax.numpy as jnp
import numpy as np
from jax import lax

D = 7168
FF = 2048
HEADS = 128
LAT = 512
ROPE = 64
TOPK = 8
EXPERTS = 16
REQ_DEV = 2
LMAX = 256
CAP = 2
TOKENS = 32
N_EP = 16


def cache_field(key):
    base = jax.random.fold_in(key, 11)
    field = jnp.clip(jax.random.normal(base, (TOKENS, LMAX, LAT + ROPE), jnp.float32), -6.0, 6.0)
    return field


def draw_kv_cache(key, part):
    return cache_field(key).astype(jnp.bfloat16)


def draw_queries(key, part):
    base = jax.random.fold_in(key, 23)
    field = jnp.clip(jax.random.normal(base, (TOKENS, HEADS, LAT + ROPE), jnp.float32), -6.0, 6.0)
    return field.astype(jnp.bfloat16)


def draw_kv_lengths(key, part):
    base = jax.random.fold_in(key, 37)
    lengths = jax.random.randint(base, (TOKENS,), max(2, LMAX // 8), LMAX + 1).astype(jnp.int32)
    return lengths.at[0].set(LMAX)


def levels(stream_key, dims, split, least, top_value):
    def one(dim, blocks):
        draws = jax.random.uniform(jax.random.fold_in(jax.random.fold_in(stream_key, 6), dim), (blocks,), jnp.float32, least / len(split), top_value / len(split))
        return jnp.repeat(jnp.exp(draws), dims[dim] // blocks).reshape((-1,) + (1,) * (len(dims) - dim - 1))

    gain = one(*split[0])
    for cut in split[1:]:
        gain = gain * one(*cut)
    return gain


def deal_out(key, own, number, rows, count, top, bound, skew):
    sequence = jax.random.permutation(key, count)
    crowded, common = shares(count, rows * top, bound, skew, True), shares(count, rows * top, bound, skew, False)
    places = jnp.arange(count)

    def named(tallies, rotation):
        used = int((tallies > 0).sum())
        fixed = max(1, used // 4)
        moved = fixed + (places - fixed + rotation * (used - fixed)) % max(1, count - fixed)
        return jnp.zeros((count,), jnp.int32).at[sequence[jnp.where(places < fixed, places, moved)]].set(jnp.asarray(tallies, jnp.int32))

    tallies = jnp.where(number % 4 == 0, named(crowded, number // 4), named(common, number - number // 4 - 1))
    mixed = jax.random.permutation(jax.random.fold_in(own, 3), count)
    donor, receiver = mixed[0:count // 2 * 2:2], mixed[1:count // 2 * 2:2]
    slack = jnp.minimum(tallies[donor] - 1, bound - tallies[receiver]) // 2
    slack = jnp.where((donor == sequence[0]) | (receiver == sequence[0]) | (tallies[receiver] == 0), 0, jnp.maximum(slack, 0))
    moved = jax.random.randint(jax.random.fold_in(own, 4), (count // 2,), 0, 1 << 20) % (slack + 1)
    tallies = tallies.at[donor].add(-moved).at[receiver].add(moved)
    items = jnp.searchsorted(jnp.cumsum(tallies), jnp.arange(rows * top), side="right").astype(jnp.int32)
    grid = items.reshape(top, rows).T
    grid = grid[jax.random.permutation(jax.random.fold_in(own, 1), rows)]
    rotation = jax.random.randint(jax.random.fold_in(own, 2), (rows, 1), 0, top)
    return jnp.take_along_axis(grid, (jnp.arange(top)[None, :] + rotation) % top, axis=1)


def shares(count, total, most, slope, full):
    weights = [(1 << 20) // math.isqrt(rank ** slope) + 1 for rank in range(1, count + 1)]
    largest = most if full else min(most, max(-(-total // count), total * weights[0] // sum(weights)))
    least = 1 if total - largest >= count - 1 else 0
    holding, rest = [largest] + [least] * (count - 1), total - largest - least * (count - 1)
    while rest > 0:
        movable = [i for i in range(1, count) if holding[i] < largest] or [i for i in range(1, count) if holding[i] < most]
        pool, budget = sum([weights[i] for i in movable]), rest
        for i in movable:
            extra = min(most - holding[i], max(1, budget * weights[i] // pool), rest)
            holding[i] = holding[i] + extra
            rest = rest - extra
    return np.array(holding)


def gaussian(rng, dims, scale, reach, pieces=(), kind=jnp.bfloat16):
    level = levels(rng, dims, pieces, -0.22, 0.18) if pieces else 1.0
    drawn = jax.random.normal(rng, dims, jnp.float32) * scale * level
    return jnp.minimum(jnp.maximum(drawn, -reach), reach).astype(kind)


def setup_inputs(seed: int = 0, part: int = 0) -> dict:
    streams_of = jax.random.split(jax.random.key(seed), 10)
    part_keys = jax.random.split(jax.random.fold_in(streams_of[9], part), 10)
    queries = draw_queries(jax.random.fold_in(jax.random.fold_in(streams_of[9], part), 71), part)
    kv_cache = draw_kv_cache(jax.random.fold_in(jax.random.fold_in(streams_of[9], part), 71), part)
    kv_lengths = draw_kv_lengths(jax.random.fold_in(jax.random.fold_in(streams_of[9], part), 71), part)
    moe_input = gaussian(part_keys[3], (TOKENS, D), 1.0, 6.0, ((0, 16),))
    expert_ids_keys = jax.random.split(jax.random.fold_in(part_keys[4], 1), TOKENS // REQ_DEV)
    expert_ids_turns = jax.random.permutation(jax.random.fold_in(part_keys[4], 3), TOKENS // REQ_DEV)
    expert_ids = jax.vmap(lambda own, number: deal_out(jax.random.fold_in(part_keys[4], 2), own, number, REQ_DEV, EXPERTS, TOPK, CAP, 2))(expert_ids_keys, expert_ids_turns).reshape((TOKENS, TOPK))
    route_weights = jnp.clip(jnp.exp(math.log(1.0) - 2.3025851 * jax.random.uniform(part_keys[5], (TOKENS, TOPK), jnp.float32) ** levels(part_keys[5], (TOKENS, TOPK), ((0, 16),), -0.2, 0.2)), 0.1, 1.0)
    w_gate = gaussian(streams_of[6], (EXPERTS * FF, D), D ** -0.5, 0.0625, ((0, 16),))
    w_up = gaussian(streams_of[7], (EXPERTS * FF, D), D ** -0.5, 0.0625, ((0, 16),))
    w_down = gaussian(streams_of[8], (EXPERTS * FF, D), FF ** -0.5, 0.125, ((0, 16),))
    return {"queries": queries, "kv_cache": kv_cache, "kv_lengths": kv_lengths, "moe_input": moe_input, "expert_ids": expert_ids, "route_weights": route_weights, "w_gate": w_gate, "w_up": w_up, "w_down": w_down}


score_scale = 192.0 ** -0.5


def reference(queries, kv_cache, kv_lengths, moe_input, expert_ids, route_weights, w_gate, w_up, w_down):
    query_wide = queries.astype(jnp.float32)
    cache_wide = kv_cache.astype(jnp.float32)
    scores = jnp.einsum("thk,tlk->thl", query_wide, cache_wide) * score_scale
    slot_index = jnp.arange(LMAX, dtype=jnp.int32)
    usable = slot_index[None, None, :] < kv_lengths[:, None, None]
    scores = jnp.where(usable, scores, -1e30)
    row_max = jnp.max(scores, axis=2, keepdims=True)
    raw_weights = jnp.where(usable, jnp.exp(scores - row_max), 0.0)
    probs = (raw_weights / jnp.sum(raw_weights, axis=2, keepdims=True)).astype(jnp.bfloat16)
    attended = jnp.einsum("thl,tlk->thk", probs.astype(jnp.float32), cache_wide[:, :, :LAT]).astype(jnp.bfloat16)

    rows_total = N_EP * CAP
    contract = (((1,), (1,)), ((), ()))

    def one_expert(expert):
        matches = expert_ids == expert
        chosen = jnp.any(matches, axis=1)
        weight = jnp.sum(jnp.where(matches, route_weights, 0.0), axis=1)
        ordering = jnp.argsort(jnp.where(chosen, 0, 1).astype(jnp.int32), stable=True)[:rows_total].astype(jnp.int32)
        picked = moe_input[ordering]
        first_row = (expert * FF).astype(jnp.int32)
        gate_rows = lax.dynamic_slice_in_dim(w_gate, first_row, FF, 0)
        up_rows = lax.dynamic_slice_in_dim(w_up, first_row, FF, 0)
        down_rows = lax.dynamic_slice_in_dim(w_down, first_row, FF, 0)
        gate_act = lax.dot_general(picked, gate_rows, contract, preferred_element_type=jnp.float32)
        up_act = lax.dot_general(picked, up_rows, contract, preferred_element_type=jnp.float32)
        hidden = (jax.nn.silu(gate_act) * up_act).astype(jnp.bfloat16)
        expert_out = jnp.dot(hidden, down_rows, preferred_element_type=jnp.float32)
        return ordering, expert_out * weight[ordering][:, None]

    orderings, outputs = lax.map(one_expert, jnp.arange(EXPERTS, dtype=jnp.int32))
    combined = jnp.zeros((moe_input.shape[0], D), jnp.float32)
    combined = combined.at[orderings.reshape(-1)].add(outputs.reshape(-1, D))
    return attended, combined.astype(jnp.bfloat16)
```

```python
import functools

import jax
import jax.numpy as jnp
from jax import lax
from jax.experimental import pallas as pl
from jax.experimental.pallas import tpu as pltpu
from jax.sharding import PartitionSpec as P

LAT = 512
EXPERTS = 16
LANES = 128
SCORE_SCALE = 192.0 ** (-0.5)
NT = (((1,), (1,)), ((), ()))
MAX_SLOTS = 14


def attend_one(query, cache, length):
    scores = lax.dot_general(query, cache, NT, preferred_element_type=jnp.float32) * SCORE_SCALE
    usable = lax.broadcasted_iota(jnp.int32, scores.shape, 1) < length
    scores = jnp.where(usable, scores, -1e30)
    row_max = jnp.max(scores, axis=1, keepdims=True)
    raw = jnp.where(usable, jnp.exp(scores - row_max), 0.0)
    probs = (raw / jnp.sum(raw, axis=1, keepdims=True)).astype(jnp.bfloat16)
    return jnp.dot(probs, cache[:, :LAT], preferred_element_type=jnp.float32)


def weight_lanes(ids, weights):
    lane = lax.broadcasted_iota(jnp.int32, (ids.shape[0], LANES), 1)
    expert, term = lane % EXPERTS, lane // EXPERTS
    dense = jnp.zeros(lane.shape, jnp.float32)
    for k in range(ids.shape[1]):
        dense += jnp.where(ids[:, k : k + 1] == expert, weights[:, k : k + 1], 0.0)
    high = dense.astype(jnp.bfloat16).astype(jnp.float32)
    rest = dense - high
    middle = rest.astype(jnp.bfloat16).astype(jnp.float32)
    low = rest - middle
    chosen = jnp.where(term == 0, high, jnp.where(term == 1, middle, low))
    return jnp.where(term < 3, chosen, 0.0).astype(jnp.bfloat16)


def kernel(
    n,
    slots,
    block,
    lengths,
    x_ref,
    ids_ref,
    route_ref,
    q_hbm,
    kv_hbm,
    wg_hbm,
    wu_hbm,
    wd_hbm,
    att_ref,
    out_ref,
    q_v,
    kv_v,
    ring,
    gathered,
    wide,
    xb,
    hid,
    mine,
    pair_out,
    pair_in,
    cross_out,
    cross_in,
    ring_sem,
    in_sem,
    x_send,
    x_recv,
    fwd_sem,
    pair_send,
    pair_recv,
    cross_send,
    cross_recv,
):
    me = lax.axis_index("ep")
    core = me % 2
    chip = me // 2
    chips = n // 2
    sibling = me + 1 - 2 * core
    req, width = x_ref.shape
    hidden = wg_hbm.shape[0]
    blocks = hidden // block
    cols = width // blocks
    half = chips * req
    expert = me // (n // EXPERTS)

    def peer(step):
        there = (chip + step) % chips
        return there, {"ep": there * 2 + core}

    def load_rows(source, row_block, slot):
        rows = pl.ds(pl.multiple_of(row_block * block, block), block)
        pltpu.make_async_copy(source.at[rows], ring.at[slot], ring_sem.at[slot]).start()

    def load_columns(part, slot):
        columns = pl.ds(pl.multiple_of(part * cols, LANES), cols)
        for b in range(blocks):
            pltpu.make_async_copy(
                wd_hbm.at[pl.ds(b * block, block), columns],
                ring.at[slot, :, pl.ds(b * cols, cols)],
                ring_sem.at[slot],
            ).start()

    def wait_slot(slot):
        pltpu.make_async_copy(wg_hbm.at[pl.ds(0, block)], ring.at[slot], ring_sem.at[slot]).wait()

    q_copy = pltpu.make_async_copy(q_hbm, q_v, in_sem.at[0])
    kv_copy = pltpu.make_async_copy(kv_hbm, kv_v, in_sem.at[1])
    q_copy.start()
    kv_copy.start()
    for i in range(slots):
        if i < 2 * blocks:
            load_rows(wg_hbm if i % 2 == 0 else wu_hbm, i // 2, i)
        else:
            load_columns(i - 2 * blocks, i)

    barrier = pltpu.get_barrier_semaphore()
    pl.semaphore_signal(
        barrier, inc=1, device_id={"ep": sibling}, device_id_type=pl.DeviceIdType.MESH
    )
    for step in range(1, chips):
        _, target = peer(step)
        pl.semaphore_signal(barrier, inc=1, device_id=target, device_id_type=pl.DeviceIdType.MESH)

    gathered[core, chip, :, pl.ds(0, width)] = x_ref[...]
    gathered[core, chip, :, pl.ds(width, LANES)] = weight_lanes(ids_ref[...], route_ref[...])
    pl.semaphore_wait(barrier, chips)

    def dispatch(step):
        _, target = peer(step)
        return pltpu.make_async_remote_copy(
            src_ref=gathered.at[core, chip],
            dst_ref=gathered.at[core, chip],
            send_sem=x_send,
            recv_sem=x_recv,
            device_id=target,
            device_id_type=pl.DeviceIdType.MESH,
        )

    for step in range(1, chips):
        dispatch(step).start()

    q_copy.wait()
    kv_copy.wait()
    for r in range(q_v.shape[0]):
        att_ref[r] = attend_one(q_v[r], kv_v[r], lengths[r]).astype(att_ref.dtype)

    others = gathered.at[core, pl.ds(0, chips - 1)]
    pltpu.make_async_copy(others, others, x_recv).wait()
    forward = pltpu.make_async_remote_copy(
        src_ref=gathered.at[core],
        dst_ref=gathered.at[core],
        send_sem=fwd_sem.at[0],
        recv_sem=fwd_sem.at[1],
        device_id={"ep": sibling},
        device_id_type=pl.DeviceIdType.MESH,
    )
    forward.start()
    for q in range(chips):
        wide[pl.ds(q * req, req), :] = gathered[core, q].astype(jnp.float32)
    forward.wait()
    for q in range(chips):
        wide[pl.ds(half + q * req, req), :] = gathered[1 - core, q].astype(jnp.float32)
    xb[...] = wide[:, :width].astype(jnp.bfloat16)
    lanes = wide[:, width:]
    lane = lax.broadcasted_iota(jnp.int32, lanes.shape, 1)
    share = jnp.sum(jnp.where(lane % EXPERTS == expert, lanes, 0.0), axis=1, keepdims=True)

    def gate_up(b, carry):
        first = (2 * b) % slots
        second = (2 * b + 1) % slots
        wait_slot(first)
        gate = lax.dot_general(xb[...], ring[first], NT, preferred_element_type=jnp.float32)
        wait_slot(second)
        up = lax.dot_general(xb[...], ring[second], NT, preferred_element_type=jnp.float32)
        hid[b] = (gate / (1.0 + jnp.exp(-gate)) * up).astype(jnp.bfloat16)
        ahead = 2 * b + slots

        @pl.when(ahead < 2 * blocks)
        def _():
            load_rows(wg_hbm, b + slots // 2, first)
            load_rows(wu_hbm, b + slots // 2, second)

        @pl.when(jnp.logical_and(ahead >= 2 * blocks, ahead < 3 * blocks))
        def _():
            load_columns(ahead - 2 * blocks, first)

        @pl.when(jnp.logical_and(ahead >= 2 * blocks, ahead + 1 < 3 * blocks))
        def _():
            load_columns(ahead + 1 - 2 * blocks, second)

        return carry

    lax.fori_loop(0, blocks, gate_up, 0)

    def pair_copy(c):
        return pltpu.make_async_remote_copy(
            src_ref=pair_out.at[c],
            dst_ref=pair_in.at[c],
            send_sem=pair_send.at[c],
            recv_sem=pair_recv.at[c],
            device_id={"ep": sibling},
            device_id_type=pl.DeviceIdType.MESH,
        )

    def send_on(c):
        pair_copy(c).wait_recv()
        total = (mine[c] + pair_in[c].astype(jnp.float32)).astype(jnp.bfloat16)
        total = total.astype(jnp.float32)
        for q in range(chips):
            cross_out[c, q] = total[q * req : (q + 1) * req].astype(jnp.bfloat16)
        for step in range(1, chips):
            there, target = peer(step)
            pltpu.make_async_remote_copy(
                src_ref=cross_out.at[c, there],
                dst_ref=cross_in.at[c, step - 1],
                send_sem=cross_send.at[c],
                recv_sem=cross_recv.at[c],
                device_id=target,
                device_id_type=pl.DeviceIdType.MESH,
            ).start()

    def down(c, carry):
        slot = (2 * blocks + c) % slots
        wait_slot(slot)
        product = jnp.zeros((2 * half, cols), jnp.float32)
        for b in range(blocks):
            product += jnp.dot(
                hid[b], ring[slot, :, b * cols : (b + 1) * cols], preferred_element_type=jnp.float32
            )
        product = product * share
        mine[c] = product[:half]
        pair_out[c] = product[half:].astype(jnp.bfloat16)
        pair_copy(c).start()

        @pl.when(c > 0)
        def _():
            send_on(c - 1)

        ahead = c + slots

        @pl.when(ahead < blocks)
        def _():
            load_columns(ahead, slot)

        return carry

    lax.fori_loop(0, blocks, down, 0)
    send_on(blocks - 1)

    for c in range(blocks):
        arrived = cross_in.at[c]
        pltpu.make_async_copy(arrived, arrived, cross_recv.at[c]).wait()
        total = cross_out[c, chip].astype(jnp.float32)
        for s in range(chips - 1):
            total += cross_in[c, s].astype(jnp.float32)
        out_ref[:, pl.ds(c * cols, cols)] = total.astype(out_ref.dtype)

    pltpu.make_async_copy(others, others, x_send).wait()
    for c in range(blocks):
        pair_copy(c).wait_send()
        sent = cross_out.at[c, pl.ds(0, chips - 1)]
        pltpu.make_async_copy(sent, sent, cross_send.at[c]).wait()


def local(n, queries, kv_cache, kv_lengths, moe_input, expert_ids, route_weights, wg, wu, wd):
    req, width = moe_input.shape
    hidden = wg.shape[0]
    block = min(256, hidden)
    blocks = hidden // block
    cols = width // blocks
    slots = min(MAX_SLOTS, 2 * ((3 * blocks) // 2))
    slots = max(slots, 2)
    chips = n // 2
    rows = n * req
    half = rows // 2
    bf16, f32 = jnp.bfloat16, jnp.float32
    vmem = pl.BlockSpec(memory_space=pltpu.VMEM)
    hbm = pl.BlockSpec(memory_space=pl.ANY)
    return pl.pallas_call(
        functools.partial(kernel, n, slots, block),
        out_shape=(
            jax.ShapeDtypeStruct(queries.shape[:2] + (LAT,), bf16),
            jax.ShapeDtypeStruct((req, width), bf16),
        ),
        in_specs=[pl.BlockSpec(memory_space=pltpu.SMEM)] + [vmem] * 3 + [hbm] * 5,
        out_specs=(vmem, vmem),
        scratch_shapes=[
            pltpu.VMEM(queries.shape, bf16),
            pltpu.VMEM(kv_cache.shape, bf16),
            pltpu.VMEM((slots, block, width), bf16),
            pltpu.VMEM((2, chips, req, width + LANES), bf16),
            pltpu.VMEM((rows, width + LANES), f32),
            pltpu.VMEM((rows, width), bf16),
            pltpu.VMEM((blocks, rows, block), bf16),
            pltpu.VMEM((blocks, half, cols), f32),
            pltpu.VMEM((blocks, half, cols), bf16),
            pltpu.VMEM((blocks, half, cols), bf16),
            pltpu.VMEM((blocks, chips, req, cols), bf16),
            pltpu.VMEM((blocks, chips - 1, req, cols), bf16),
            pltpu.SemaphoreType.DMA((slots,)),
            pltpu.SemaphoreType.DMA((2,)),
            pltpu.SemaphoreType.DMA,
            pltpu.SemaphoreType.DMA,
            pltpu.SemaphoreType.DMA((2,)),
            pltpu.SemaphoreType.DMA((blocks,)),
            pltpu.SemaphoreType.DMA((blocks,)),
            pltpu.SemaphoreType.DMA((blocks,)),
            pltpu.SemaphoreType.DMA((blocks,)),
        ],
        compiler_params=pltpu.CompilerParams(
            collective_id=0, has_side_effects=True, vmem_limit_bytes=58 * 2**20
        ),
    )(kv_lengths, moe_input, expert_ids, route_weights, queries, kv_cache, wg, wu, wd)


def solution(mesh):
    in_specs = (
        P(("groups", "ep"), None, None),
        P(("groups", "ep"), None, None),
        P(("groups", "ep")),
        P(("groups", "ep"), None),
        P(("groups", "ep"), None),
        P(("groups", "ep"), None),
        P("ep", None),
        P("ep", None),
        P("ep", None),
    )
    out_specs = (P(("groups", "ep"), None, None), P(("groups", "ep"), None))
    n = mesh.shape["ep"]
    return jax.shard_map(
        functools.partial(local, n), mesh=mesh, in_specs=in_specs, out_specs=out_specs, check_vma=False
    )
```

```python
import functools

import jax
import jax.numpy as jnp
from jax import lax
from jax.experimental import pallas as pl
from jax.experimental.pallas import tpu as pltpu
from jax.sharding import PartitionSpec as P

LAT = 512
EXPERTS = 16
LANES = 128
SCORE_SCALE = 192.0 ** (-0.5)
NT = (((1,), (1,)), ((), ()))
TN = (((0,), (0,)), ((), ()))
MAX_SLOTS = 14


def attend_one(query, cache, length):
    scores = lax.dot_general(query, cache, TN, preferred_element_type=jnp.float32) * SCORE_SCALE
    usable = lax.broadcasted_iota(jnp.int32, scores.shape, 1) < length
    scores = jnp.where(usable, scores, -1e30)
    row_max = jnp.max(scores, axis=1, keepdims=True)
    raw = jnp.where(usable, jnp.exp(scores - row_max), 0.0)
    probs = (raw / jnp.sum(raw, axis=1, keepdims=True)).astype(jnp.bfloat16)
    return lax.dot_general(probs, cache[:LAT], NT, preferred_element_type=jnp.float32)


def weight_lanes(ids, weights):
    lane = lax.broadcasted_iota(jnp.int32, (ids.shape[0], LANES), 1)
    expert, term = lane % EXPERTS, lane // EXPERTS
    dense = jnp.zeros(lane.shape, jnp.float32)
    for k in range(ids.shape[1]):
        dense += jnp.where(ids[:, k : k + 1] == expert, weights[:, k : k + 1], 0.0)
    high = dense.astype(jnp.bfloat16).astype(jnp.float32)
    rest = dense - high
    middle = rest.astype(jnp.bfloat16).astype(jnp.float32)
    low = rest - middle
    chosen = jnp.where(term == 0, high, jnp.where(term == 1, middle, low))
    return jnp.where(term < 3, chosen, 0.0).astype(jnp.bfloat16)


def kernel(
    n,
    slots,
    block,
    lengths,
    x_ref,
    ids_ref,
    route_ref,
    q_hbm,
    kv_hbm,
    wg_hbm,
    wu_hbm,
    wd_hbm,
    att_ref,
    out_ref,
    q_v,
    kv_v,
    ring,
    gathered,
    wide,
    xb,
    hid,
    mine,
    pair_out,
    pair_in,
    cross_out,
    cross_in,
    ring_sem,
    in_sem,
    x_send,
    x_recv,
    fwd_sem,
    pair_send,
    pair_recv,
    cross_send,
    cross_recv,
):
    me = lax.axis_index("ep")
    core = me % 2
    chip = me // 2
    chips = n // 2
    sibling = me + 1 - 2 * core
    req, width = x_ref.shape
    hidden = wg_hbm.shape[0]
    blocks = hidden // block
    cols = width // blocks
    half = chips * req
    expert = me // (n // EXPERTS)

    def peer(step):
        there = (chip + step) % chips
        return there, {"ep": there * 2 + core}

    def load_rows(source, row_block, slot):
        rows = pl.ds(pl.multiple_of(row_block * block, block), block)
        pltpu.make_async_copy(source.at[rows], ring.at[slot], ring_sem.at[slot]).start()

    def load_columns(part, slot):
        columns = pl.ds(pl.multiple_of(part * cols, LANES), cols)
        for b in range(blocks):
            pltpu.make_async_copy(
                wd_hbm.at[pl.ds(b * block, block), columns],
                ring.at[slot, :, pl.ds(b * cols, cols)],
                ring_sem.at[slot],
            ).start()

    def wait_slot(slot):
        pltpu.make_async_copy(wg_hbm.at[pl.ds(0, block)], ring.at[slot], ring_sem.at[slot]).wait()

    q_copy = pltpu.make_async_copy(q_hbm, q_v, in_sem.at[0])
    kv_copy = pltpu.make_async_copy(kv_hbm, kv_v, in_sem.at[1])
    q_copy.start()
    kv_copy.start()
    for i in range(slots):
        if i < 2 * blocks:
            load_rows(wg_hbm if i % 2 == 0 else wu_hbm, i // 2, i)
        else:
            load_columns(i - 2 * blocks, i)

    barrier = pltpu.get_barrier_semaphore()
    pl.semaphore_signal(
        barrier, inc=1, device_id={"ep": sibling}, device_id_type=pl.DeviceIdType.MESH
    )
    for step in range(1, chips):
        _, target = peer(step)
        pl.semaphore_signal(barrier, inc=1, device_id=target, device_id_type=pl.DeviceIdType.MESH)

    gathered[core, chip, :, pl.ds(0, width)] = x_ref[...]
    gathered[core, chip, :, pl.ds(width, LANES)] = weight_lanes(ids_ref[...], route_ref[...])
    pl.semaphore_wait(barrier, chips)

    def dispatch(step):
        _, target = peer(step)
        return pltpu.make_async_remote_copy(
            src_ref=gathered.at[core, chip],
            dst_ref=gathered.at[core, chip],
            send_sem=x_send,
            recv_sem=x_recv,
            device_id=target,
            device_id_type=pl.DeviceIdType.MESH,
        )

    for step in range(1, chips):
        dispatch(step).start()

    q_copy.wait()
    kv_copy.wait()
    for r in range(q_v.shape[0]):
        att_ref[r] = attend_one(q_v[r], kv_v[r], lengths[r]).astype(att_ref.dtype)

    others = gathered.at[core, pl.ds(0, chips - 1)]
    pltpu.make_async_copy(others, others, x_recv).wait()
    forward = pltpu.make_async_remote_copy(
        src_ref=gathered.at[core],
        dst_ref=gathered.at[core],
        send_sem=fwd_sem.at[0],
        recv_sem=fwd_sem.at[1],
        device_id={"ep": sibling},
        device_id_type=pl.DeviceIdType.MESH,
    )
    forward.start()
    for q in range(chips):
        wide[pl.ds(q * req, req), :] = gathered[core, q].astype(jnp.float32)
    forward.wait()
    for q in range(chips):
        wide[pl.ds(half + q * req, req), :] = gathered[1 - core, q].astype(jnp.float32)
    xb[...] = wide[:, :width].astype(jnp.bfloat16)
    lanes = wide[:, width:]
    lane = lax.broadcasted_iota(jnp.int32, lanes.shape, 1)
    share = jnp.sum(jnp.where(lane % EXPERTS == expert, lanes, 0.0), axis=1, keepdims=True)

    def gate_up(b, carry):
        first = (2 * b) % slots
        second = (2 * b + 1) % slots
        wait_slot(first)
        wait_slot(second)
        pair = ring[pl.ds(first, 2)].reshape(2 * block, width)
        both = lax.dot_general(xb[...], pair, NT, preferred_element_type=jnp.float32)
        gate, up = both[:, :block], both[:, block:]
        hid[b] = (gate / (1.0 + jnp.exp(-gate)) * up).astype(jnp.bfloat16)
        ahead = 2 * b + slots

        @pl.when(ahead < 2 * blocks)
        def _():
            load_rows(wg_hbm, b + slots // 2, first)
            load_rows(wu_hbm, b + slots // 2, second)

        @pl.when(jnp.logical_and(ahead >= 2 * blocks, ahead < 3 * blocks))
        def _():
            load_columns(ahead - 2 * blocks, first)

        @pl.when(jnp.logical_and(ahead >= 2 * blocks, ahead + 1 < 3 * blocks))
        def _():
            load_columns(ahead + 1 - 2 * blocks, second)

        return carry

    lax.fori_loop(0, blocks, gate_up, 0)

    def pair_copy(c):
        return pltpu.make_async_remote_copy(
            src_ref=pair_out.at[c],
            dst_ref=pair_in.at[c],
            send_sem=pair_send.at[c],
            recv_sem=pair_recv.at[c],
            device_id={"ep": sibling},
            device_id_type=pl.DeviceIdType.MESH,
        )

    def send_on(c):
        pair_copy(c).wait_recv()
        total = (mine[c] + pair_in[c].astype(jnp.float32)).astype(jnp.bfloat16)
        total = total.astype(jnp.float32)
        for q in range(chips):
            cross_out[c, q] = total[q * req : (q + 1) * req].astype(jnp.bfloat16)
        for step in range(1, chips):
            there, target = peer(step)
            pltpu.make_async_remote_copy(
                src_ref=cross_out.at[c, there],
                dst_ref=cross_in.at[c, step - 1],
                send_sem=cross_send.at[c],
                recv_sem=cross_recv.at[c],
                device_id=target,
                device_id_type=pl.DeviceIdType.MESH,
            ).start()

    def down(c, carry):
        slot = (2 * blocks + c) % slots
        wait_slot(slot)
        product = jnp.zeros((2 * half, cols), jnp.float32)
        for b in range(blocks):
            product += jnp.dot(
                hid[b], ring[slot, :, b * cols : (b + 1) * cols], preferred_element_type=jnp.float32
            )
        product = product * share
        mine[c] = product[:half]
        pair_out[c] = product[half:].astype(jnp.bfloat16)
        pair_copy(c).start()

        @pl.when(c > 0)
        def _():
            send_on(c - 1)

        ahead = c + slots

        @pl.when(ahead < blocks)
        def _():
            load_columns(ahead, slot)

        return carry

    lax.fori_loop(0, blocks, down, 0)
    send_on(blocks - 1)

    for c in range(blocks):
        arrived = cross_in.at[c]
        pltpu.make_async_copy(arrived, arrived, cross_recv.at[c]).wait()
        total = cross_out[c, chip].astype(jnp.float32)
        for s in range(chips - 1):
            total += cross_in[c, s].astype(jnp.float32)
        out_ref[:, pl.ds(c * cols, cols)] = total.astype(out_ref.dtype)

    pltpu.make_async_copy(others, others, x_send).wait()
    for c in range(blocks):
        pair_copy(c).wait_send()
        sent = cross_out.at[c, pl.ds(0, chips - 1)]
        pltpu.make_async_copy(sent, sent, cross_send.at[c]).wait()


def local(n, queries, kv_cache, kv_lengths, moe_input, expert_ids, route_weights, wg, wu, wd):
    heads = queries.shape[1]
    queries, kv_cache = jnp.swapaxes(queries, 1, 2), jnp.swapaxes(kv_cache, 1, 2)
    req, width = moe_input.shape
    hidden = wg.shape[0]
    block = min(256, hidden)
    blocks = hidden // block
    cols = width // blocks
    slots = min(MAX_SLOTS, 2 * ((3 * blocks) // 2))
    slots = max(slots, 2)
    chips = n // 2
    rows = n * req
    half = rows // 2
    bf16, f32 = jnp.bfloat16, jnp.float32
    vmem = pl.BlockSpec(memory_space=pltpu.VMEM)
    hbm = pl.BlockSpec(memory_space=pl.ANY)
    return pl.pallas_call(
        functools.partial(kernel, n, slots, block),
        out_shape=(
            jax.ShapeDtypeStruct((queries.shape[0], heads, LAT), bf16),
            jax.ShapeDtypeStruct((req, width), bf16),
        ),
        in_specs=[pl.BlockSpec(memory_space=pltpu.SMEM)] + [vmem] * 3 + [hbm] * 5,
        out_specs=(vmem, vmem),
        scratch_shapes=[
            pltpu.VMEM(queries.shape, bf16),
            pltpu.VMEM(kv_cache.shape, bf16),
            pltpu.VMEM((slots, block, width), bf16),
            pltpu.VMEM((2, chips, req, width + LANES), bf16),
            pltpu.VMEM((rows, width + LANES), f32),
            pltpu.VMEM((rows, width), bf16),
            pltpu.VMEM((blocks, rows, block), bf16),
            pltpu.VMEM((blocks, half, cols), f32),
            pltpu.VMEM((blocks, half, cols), bf16),
            pltpu.VMEM((blocks, half, cols), bf16),
            pltpu.VMEM((blocks, chips, req, cols), bf16),
            pltpu.VMEM((blocks, chips - 1, req, cols), bf16),
            pltpu.SemaphoreType.DMA((slots,)),
            pltpu.SemaphoreType.DMA((2,)),
            pltpu.SemaphoreType.DMA,
            pltpu.SemaphoreType.DMA,
            pltpu.SemaphoreType.DMA((2,)),
            pltpu.SemaphoreType.DMA((blocks,)),
            pltpu.SemaphoreType.DMA((blocks,)),
            pltpu.SemaphoreType.DMA((blocks,)),
            pltpu.SemaphoreType.DMA((blocks,)),
        ],
        compiler_params=pltpu.CompilerParams(
            collective_id=0, has_side_effects=True, vmem_limit_bytes=58 * 2**20
        ),
    )(kv_lengths, moe_input, expert_ids, route_weights, queries, kv_cache, wg, wu, wd)


def solution(mesh):
    in_specs = (
        P(("groups", "ep"), None, None),
        P(("groups", "ep"), None, None),
        P(("groups", "ep")),
        P(("groups", "ep"), None),
        P(("groups", "ep"), None),
        P(("groups", "ep"), None),
        P("ep", None),
        P("ep", None),
        P("ep", None),
    )
    out_specs = (P(("groups", "ep"), None, None), P(("groups", "ep"), None))
    n = mesh.shape["ep"]
    return jax.shard_map(
        functools.partial(local, n), mesh=mesh, in_specs=in_specs, out_specs=out_specs, check_vma=False
    )
```

```python
import functools

import jax
import jax.numpy as jnp
from jax import lax
from jax.experimental import pallas as pl
from jax.experimental.pallas import tpu as pltpu
from jax.sharding import PartitionSpec as P

LAT = 512
EXPERTS = 16
LANES = 128
SCORE_SCALE = 192.0 ** (-0.5)
NT = (((1,), (1,)), ((), ()))
TN = (((0,), (0,)), ((), ()))
ROW_SLOTS = 8
DOWN_SLOTS = 6


def attend_one(query, cache, length):
    scores = lax.dot_general(query, cache, TN, preferred_element_type=jnp.float32) * SCORE_SCALE
    usable = lax.broadcasted_iota(jnp.int32, scores.shape, 1) < length
    scores = jnp.where(usable, scores, -1e30)
    row_max = jnp.max(scores, axis=1, keepdims=True)
    raw = jnp.where(usable, jnp.exp(scores - row_max), 0.0)
    probs = (raw / jnp.sum(raw, axis=1, keepdims=True)).astype(jnp.bfloat16)
    return lax.dot_general(probs, cache[:LAT], NT, preferred_element_type=jnp.float32)


def weight_lanes(ids, weights):
    lane = lax.broadcasted_iota(jnp.int32, (ids.shape[0], LANES), 1)
    expert, term = lane % EXPERTS, lane // EXPERTS
    dense = jnp.zeros(lane.shape, jnp.float32)
    for k in range(ids.shape[1]):
        dense += jnp.where(ids[:, k : k + 1] == expert, weights[:, k : k + 1], 0.0)
    high = dense.astype(jnp.bfloat16).astype(jnp.float32)
    rest = dense - high
    middle = rest.astype(jnp.bfloat16).astype(jnp.float32)
    low = rest - middle
    chosen = jnp.where(term == 0, high, jnp.where(term == 1, middle, low))
    return jnp.where(term < 3, chosen, 0.0).astype(jnp.bfloat16)


def kernel(
    n,
    block,
    lengths,
    x_ref,
    ids_ref,
    route_ref,
    q_hbm,
    kv_hbm,
    wg_hbm,
    wu_hbm,
    wd_hbm,
    att_ref,
    out_ref,
    q_v,
    kv_v,
    ring,
    down_ring,
    gathered,
    wide,
    xb,
    hid,
    mine,
    pair_out,
    pair_in,
    cross_out,
    cross_in,
    ring_sem,
    down_sem,
    in_sem,
    x_send,
    x_recv,
    fwd_sem,
    pair_send,
    pair_recv,
    cross_send,
    cross_recv,
):
    me = lax.axis_index("ep")
    core = me % 2
    chip = me // 2
    chips = n // 2
    sibling = me + 1 - 2 * core
    req, width = x_ref.shape
    hidden = wg_hbm.shape[0]
    blocks = hidden // block
    cols = width // blocks
    slots, down_slots = ring.shape[0], down_ring.shape[0]
    half = chips * req
    expert = me // (n // EXPERTS)

    def peer(step):
        there = (chip + step) % chips
        return there, {"ep": there * 2 + core}

    barrier = pltpu.get_barrier_semaphore()
    pl.semaphore_signal(
        barrier, inc=1, device_id={"ep": sibling}, device_id_type=pl.DeviceIdType.MESH
    )
    for step in range(1, chips):
        _, target = peer(step)
        pl.semaphore_signal(barrier, inc=1, device_id=target, device_id_type=pl.DeviceIdType.MESH)

    def load_rows(source, row_block, slot):
        rows = pl.ds(pl.multiple_of(row_block * block, block), block)
        pltpu.make_async_copy(source.at[rows], ring.at[slot], ring_sem.at[slot]).start()

    def column_copy(part, slot):
        columns = pl.ds(pl.multiple_of(part * cols, LANES), cols)
        return pltpu.make_async_copy(
            wd_hbm.at[:, :, columns], down_ring.at[slot], down_sem.at[slot]
        )

    def wait_slot(slot):
        pltpu.make_async_copy(wg_hbm.at[pl.ds(0, block)], ring.at[slot], ring_sem.at[slot]).wait()

    q_copy = pltpu.make_async_copy(q_hbm, q_v, in_sem.at[0])
    kv_copy = pltpu.make_async_copy(kv_hbm, kv_v, in_sem.at[1])
    q_copy.start()
    kv_copy.start()
    for i in range(slots):
        load_rows(wg_hbm if i % 2 == 0 else wu_hbm, i // 2, i)
    for c in range(down_slots):
        column_copy(c, c).start()

    gathered[core, chip, :, pl.ds(0, width)] = x_ref[...]
    gathered[core, chip, :, pl.ds(width, LANES)] = weight_lanes(ids_ref[...], route_ref[...])
    pl.semaphore_wait(barrier, chips)

    def dispatch(step):
        _, target = peer(step)
        return pltpu.make_async_remote_copy(
            src_ref=gathered.at[core, chip],
            dst_ref=gathered.at[core, chip],
            send_sem=x_send,
            recv_sem=x_recv,
            device_id=target,
            device_id_type=pl.DeviceIdType.MESH,
        )

    for step in range(1, chips):
        dispatch(step).start()

    q_copy.wait()
    kv_copy.wait()
    for r in range(q_v.shape[0]):
        att_ref[r] = attend_one(q_v[r], kv_v[r], lengths[r]).astype(att_ref.dtype)

    others = gathered.at[core, pl.ds(0, chips - 1)]
    pltpu.make_async_copy(others, others, x_recv).wait()
    forward = pltpu.make_async_remote_copy(
        src_ref=gathered.at[core],
        dst_ref=gathered.at[core],
        send_sem=fwd_sem.at[0],
        recv_sem=fwd_sem.at[1],
        device_id={"ep": sibling},
        device_id_type=pl.DeviceIdType.MESH,
    )
    forward.start()
    for q in range(chips):
        wide[pl.ds(q * req, req), :] = gathered[core, q].astype(jnp.float32)
    forward.wait()
    for q in range(chips):
        wide[pl.ds(half + q * req, req), :] = gathered[1 - core, q].astype(jnp.float32)
    xb[...] = wide[:, :width].astype(jnp.bfloat16)
    lanes = wide[:, width:]
    lane = lax.broadcasted_iota(jnp.int32, lanes.shape, 1)
    share = jnp.sum(jnp.where(lane % EXPERTS == expert, lanes, 0.0), axis=1, keepdims=True)

    def gate_up(b, carry):
        first = (2 * b) % slots
        second = (2 * b + 1) % slots
        wait_slot(first)
        wait_slot(second)
        pair = ring[pl.ds(first, 2)].reshape(2 * block, width)
        both = lax.dot_general(pair, xb[...], NT, preferred_element_type=jnp.float32).T
        gate, up = both[:, :block], both[:, block:]
        hid[b] = (gate / (1.0 + jnp.exp(-gate)) * up).astype(jnp.bfloat16)
        ahead = 2 * b + slots

        @pl.when(ahead < 2 * blocks)
        def _():
            load_rows(wg_hbm, b + slots // 2, first)
            load_rows(wu_hbm, b + slots // 2, second)

        return carry

    lax.fori_loop(0, blocks, gate_up, 0)

    def pair_copy(c):
        return pltpu.make_async_remote_copy(
            src_ref=pair_out.at[c],
            dst_ref=pair_in.at[c],
            send_sem=pair_send.at[c],
            recv_sem=pair_recv.at[c],
            device_id={"ep": sibling},
            device_id_type=pl.DeviceIdType.MESH,
        )

    def send_on(c):
        pair_copy(c).wait_recv()
        total = mine[c] + pair_in[c].astype(jnp.float32)
        for q in range(chips):
            cross_out[c, q] = total[q * req : (q + 1) * req].astype(jnp.bfloat16)
        for step in range(1, chips):
            there, target = peer(step)
            pltpu.make_async_remote_copy(
                src_ref=cross_out.at[c, there],
                dst_ref=cross_in.at[c, step - 1],
                send_sem=cross_send.at[c],
                recv_sem=cross_recv.at[c],
                device_id=target,
                device_id_type=pl.DeviceIdType.MESH,
            ).start()

    def down(c, carry):
        slot = c % down_slots
        column_copy(c, slot).wait()
        product = jnp.zeros((2 * half, cols), jnp.float32)
        for b in range(blocks):
            product += jnp.dot(
                hid[b], down_ring[slot, b], preferred_element_type=jnp.float32
            )
        product = product * share
        mine[c] = product[:half]
        pair_out[c] = product[half:].astype(jnp.bfloat16)
        pair_copy(c).start()

        @pl.when(c > 0)
        def _():
            send_on(c - 1)

        ahead = c + down_slots

        @pl.when(ahead < blocks)
        def _():
            column_copy(ahead, slot).start()

        return carry

    lax.fori_loop(0, blocks, down, 0)
    send_on(blocks - 1)

    for c in range(blocks):
        arrived = cross_in.at[c]
        pltpu.make_async_copy(arrived, arrived, cross_recv.at[c]).wait()
        total = cross_out[c, chip].astype(jnp.float32)
        for s in range(chips - 1):
            total += cross_in[c, s].astype(jnp.float32)
        out_ref[:, pl.ds(c * cols, cols)] = total.astype(out_ref.dtype)

    pltpu.make_async_copy(others, others, x_send).wait()
    for c in range(blocks):
        pair_copy(c).wait_send()
        sent = cross_out.at[c, pl.ds(0, chips - 1)]
        pltpu.make_async_copy(sent, sent, cross_send.at[c]).wait()


def local(n, queries, kv_cache, kv_lengths, moe_input, expert_ids, route_weights, wg, wu, wd):
    heads = queries.shape[1]
    queries, kv_cache = jnp.swapaxes(queries, 1, 2), jnp.swapaxes(kv_cache, 1, 2)
    req, width = moe_input.shape
    hidden = wg.shape[0]
    block = min(256, hidden)
    blocks = hidden // block
    cols = width // blocks
    slots, down_slots = 2 * min(ROW_SLOTS // 2, blocks), min(DOWN_SLOTS, blocks)
    chips = n // 2
    rows = n * req
    half = rows // 2
    bf16, f32 = jnp.bfloat16, jnp.float32
    vmem = pl.BlockSpec(memory_space=pltpu.VMEM)
    hbm = pl.BlockSpec(memory_space=pl.ANY)
    return pl.pallas_call(
        functools.partial(kernel, n, block),
        out_shape=(
            jax.ShapeDtypeStruct((queries.shape[0], heads, LAT), bf16),
            jax.ShapeDtypeStruct((req, width), bf16),
        ),
        in_specs=[pl.BlockSpec(memory_space=pltpu.SMEM)] + [vmem] * 3 + [hbm] * 5,
        out_specs=(vmem, vmem),
        scratch_shapes=[
            pltpu.VMEM(queries.shape, bf16),
            pltpu.VMEM(kv_cache.shape, bf16),
            pltpu.VMEM((slots, block, width), bf16),
            pltpu.VMEM((down_slots, blocks, block, cols), bf16),
            pltpu.VMEM((2, chips, req, width + LANES), bf16),
            pltpu.VMEM((rows, width + LANES), f32),
            pltpu.VMEM((rows, width), bf16),
            pltpu.VMEM((blocks, rows, block), bf16),
            pltpu.VMEM((blocks, half, cols), f32),
            pltpu.VMEM((blocks, half, cols), bf16),
            pltpu.VMEM((blocks, half, cols), bf16),
            pltpu.VMEM((blocks, chips, req, cols), bf16),
            pltpu.VMEM((blocks, chips - 1, req, cols), bf16),
            pltpu.SemaphoreType.DMA((slots,)),
            pltpu.SemaphoreType.DMA((down_slots,)),
            pltpu.SemaphoreType.DMA((2,)),
            pltpu.SemaphoreType.DMA,
            pltpu.SemaphoreType.DMA,
            pltpu.SemaphoreType.DMA((2,)),
            pltpu.SemaphoreType.DMA((blocks,)),
            pltpu.SemaphoreType.DMA((blocks,)),
            pltpu.SemaphoreType.DMA((blocks,)),
            pltpu.SemaphoreType.DMA((blocks,)),
        ],
        compiler_params=pltpu.CompilerParams(
            collective_id=0, has_side_effects=True, vmem_limit_bytes=58 * 2**20
        ),
    )(
        kv_lengths, moe_input, expert_ids, route_weights, queries, kv_cache, wg, wu,
        wd.reshape(blocks, block, width),
    )


def solution(mesh):
    in_specs = (
        P(("groups", "ep"), None, None),
        P(("groups", "ep"), None, None),
        P(("groups", "ep")),
        P(("groups", "ep"), None),
        P(("groups", "ep"), None),
        P(("groups", "ep"), None),
        P("ep", None),
        P("ep", None),
        P("ep", None),
    )
    out_specs = (P(("groups", "ep"), None, None), P(("groups", "ep"), None))
    n = mesh.shape["ep"]
    return jax.shard_map(
        functools.partial(local, n), mesh=mesh, in_specs=in_specs, out_specs=out_specs, check_vma=False
    )
```
